32 devices in a mesh: seq: 16 (over z, y, core), section: 2 (over x).
Axes of the slice: x: 2, y: 2, z: 4, core: 2. Of those that a mesh axis runs over, the one named last changes fastest.
Arguments:
- query_rows: bfloat16 [8192, 4096], P('seq', 'section'), may hold values from -6 to 6
- key_rows: bfloat16 [8192, 4096], P('seq', 'section'), may hold values from -6 to 6
- value_rows: bfloat16 [8192, 4096], P('seq', 'section'), may hold values from -6 to 6
- log_decay: float32 [8192, 32], P('seq', 'section'), may hold values from -1 to 0
- lengths: int32 [32], replicated, may hold values from 1 to 4096, as said below
- norm_gain: float32 [4096], P('section'), may hold values from 0.1 to 1.9
Outputs:
- next_input: bfloat16 [8192, 4096], P(('seq', 'section'))
The draws below stay inside these ranges and needn't reach their ends.
Inputs may be any that keep to these rules, and one draw needn't show every extreme that they name: The lengths of 32 documents in order, summing to 8192; the document at index (31) // 2 is the longest, exactly 4096 tokens, and starts at token 2048.
All inputs are finite; a program needn't handle non-finite values.
Results may differ from the reference program's by a relative error of at most 0.0058.
Values may be sent and summed in bfloat16 or wider, within the bound.
A program may use at most 64 MiB of HBM per device.

```python
import math
import jax
import jax.numpy as jnp
from jax import lax

ATTENTION_PLANES = 32
DH = 128
TOK_DEV = 512
DOCS = 32
SEQUENCE_SYMBOLS = 8192


def split_span(key, total, pieces):
    if pieces == 1:
        return jnp.full((1,), total, jnp.int32)
    shuffled = jax.random.permutation(key, total - 1).astype(jnp.int32)
    cut_points = jnp.sort(shuffled[:pieces - 1]) + 1
    bounds = jnp.concatenate([jnp.zeros((1,), jnp.int32), cut_points.astype(jnp.int32), jnp.full((1,), total, jnp.int32)])
    return (bounds[1:] - bounds[:-1]).astype(jnp.int32)


def draw_lengths(key, part):
    half_length = SEQUENCE_SYMBOLS // 2
    quarter_length = SEQUENCE_SYMBOLS // 4
    before_docs = (DOCS - 1) // 2
    after_docs = DOCS - 1 - before_docs
    after_total = SEQUENCE_SYMBOLS - half_length - quarter_length
    before_lengths = split_span(jax.random.fold_in(key, 11), quarter_length, before_docs)
    after_lengths = split_span(jax.random.fold_in(key, 12), after_total, after_docs)
    return jnp.concatenate([before_lengths, jnp.full((1,), half_length, jnp.int32), after_lengths]).astype(jnp.int32)


def draw_log_decay(key, part):
    lookup_vector_matrix = jax.random.split(key, 7)
    blocks = SEQUENCE_SYMBOLS // TOK_DEV
    fast_share = 0.5
    fast_heads = jax.random.bernoulli(lookup_vector_matrix[0], fast_share, (1, ATTENTION_PLANES))
    fast_rate = 1.0 / jax.random.uniform(lookup_vector_matrix[1], (1, ATTENTION_PLANES), jnp.float32, 30.0, 50.0)
    slow_rate = math.log(10.0) / SEQUENCE_SYMBOLS * jax.random.uniform(lookup_vector_matrix[2], (1, ATTENTION_PLANES), jnp.float32, 0.1, 0.5)
    reference_fading_speed = jnp.where(fast_heads, fast_rate, slow_rate)
    segment_scaling_factor = jnp.exp(jax.random.uniform(lookup_vector_matrix[3], (blocks, ATTENTION_PLANES), jnp.float32, -math.log(2.0), math.log(2.0)))
    segment_scaling_factor = jnp.repeat(segment_scaling_factor, TOK_DEV, axis=0)
    rough_estimate_output = jax.random.uniform(lookup_vector_matrix[4], (SEQUENCE_SYMBOLS, ATTENTION_PLANES), jnp.float32, 0.5, 1.5)
    window_clusters = jax.random.bernoulli(lookup_vector_matrix[5], 2.0 / SEQUENCE_SYMBOLS, (SEQUENCE_SYMBOLS, ATTENTION_PLANES)).astype(jnp.float32)
    window_span = jax.random.uniform(lookup_vector_matrix[6], (SEQUENCE_SYMBOLS, ATTENTION_PLANES), jnp.float32, 0.22, 0.69)
    return -(reference_fading_speed * segment_scaling_factor * rough_estimate_output + window_clusters * window_span)


def shard_levels(stream_key, dims, cuts, least, largest):
    factor_of = 1.0
    for axis_at, blocks in cuts:
        draws = jax.random.uniform(jax.random.fold_in(jax.random.fold_in(stream_key, 6), axis_at), (blocks,), jnp.float32, least / len(cuts), largest / len(cuts))
        factor_of = factor_of * jnp.repeat(jnp.exp(draws), dims[axis_at] // blocks).reshape((-1,) + (1,) * (len(dims) - 1 - axis_at))
    return factor_of


def scatter_about(stream_key, extent, scale, bound, cuts=(), kind=jnp.bfloat16):
    drawn = scale * jax.random.normal(stream_key, extent, jnp.float32)
    if cuts:
        drawn = drawn * shard_levels(stream_key, extent, cuts, -0.22, 0.18)
    return jnp.clip(drawn, -bound, bound).astype(kind)


def setup_inputs(seed: int = 0) -> dict:
    arg_keys = jax.random.split(jax.random.key(seed), 7)
    return {
        "query_rows": scatter_about(arg_keys[0], (SEQUENCE_SYMBOLS, ATTENTION_PLANES * DH), 1.0, 6.0, ((0, 16), (1, 2))),
        "key_rows": scatter_about(arg_keys[1], (SEQUENCE_SYMBOLS, ATTENTION_PLANES * DH), 1.0, 6.0, ((0, 16), (1, 2))),
        "value_rows": scatter_about(arg_keys[2], (SEQUENCE_SYMBOLS, ATTENTION_PLANES * DH), 1.0, 6.0, ((0, 16), (1, 2))),
        "log_decay": draw_log_decay(jax.random.fold_in(arg_keys[6], 71), 0),
        "lengths": draw_lengths(jax.random.fold_in(arg_keys[6], 71), 0),
        "norm_gain": jnp.clip(1.0 + 0.18 * jax.random.normal(arg_keys[5], (ATTENTION_PLANES * DH,), jnp.float32), 0.1, 1.9),
    }


def block_terms(queries, key_block, value_block, decay_block, doc_ids, prev_doc):
    tok_rows = queries.shape[0]
    head_size = queries.shape[2]
    scale_factor = 1.0 / math.sqrt(head_size)
    cumulative = jnp.cumsum(decay_block, axis=0)
    position = jnp.arange(tok_rows, dtype=jnp.int32)
    allowed = (position[:, None] >= position[None, :]) & (doc_ids[:, None] == doc_ids[None, :])
    scores = jnp.einsum('thd,uhd->htu', queries.astype(jnp.float32), key_block.astype(jnp.float32))
    log_gap = cumulative.T[:, :, None] - cumulative.T[:, None, :]
    safe_gap = jnp.where(allowed[None], log_gap, 0.0)
    weights = jnp.where(allowed[None], scores * scale_factor * jnp.exp(safe_gap), 0.0).astype(jnp.bfloat16)
    within = jnp.einsum('htu,uhd->thd', weights.astype(jnp.float32), value_block.astype(jnp.float32))
    end_log = cumulative[-1]
    in_last = (doc_ids == doc_ids[-1]).astype(jnp.float32)
    key_scale = jnp.exp(end_log[None, :] - cumulative) * in_last[:, None]
    decayed_keys = (key_block.astype(jnp.float32) * key_scale[:, :, None]).astype(jnp.bfloat16)
    block_state = jnp.einsum('thd,the->hde', decayed_keys.astype(jnp.float32), value_block.astype(jnp.float32))
    opened = (doc_ids[-1] != prev_doc).astype(jnp.float32)
    decayed_queries = (queries.astype(jnp.float32) * (jnp.exp(cumulative) * scale_factor)[:, :, None]).astype(jnp.bfloat16)
    carried = (doc_ids == prev_doc).astype(jnp.float32)
    return (within, decayed_queries, carried, end_log, opened, block_state)

def finish(within, decayed_queries, carried, incoming, gain_heads):
    incoming_low = incoming.astype(jnp.bfloat16)
    carried_out = jnp.einsum('thd,hde->the', decayed_queries.astype(jnp.float32), incoming_low.astype(jnp.float32))
    attention = within + carried[:, None, None] * carried_out
    mean_square = lax.optimization_barrier(jnp.mean(attention * attention, axis=-1, keepdims=True))
    normed = attention * lax.rsqrt(mean_square + 1e-05) * gain_heads[None]
    return normed.astype(jnp.bfloat16)

def reference(query_rows, key_rows, value_rows, log_decay, lengths, norm_gain):
    blocks = SEQUENCE_SYMBOLS // TOK_DEV
    doc_ends = jnp.cumsum(lengths).astype(jnp.int32)
    positions = jnp.arange(SEQUENCE_SYMBOLS, dtype=jnp.int32)
    doc_ids = lax.optimization_barrier(jnp.sum((doc_ends[None, :] <= positions[:, None]).astype(jnp.int32), axis=1)).astype(jnp.int32)
    first_rows = jnp.arange(blocks, dtype=jnp.int32) * TOK_DEV
    prev_docs = lax.optimization_barrier(jnp.sum((doc_ends[None, :] <= (first_rows - 1)[:, None]).astype(jnp.int32), axis=1)).astype(jnp.int32)
    gain_heads = norm_gain.reshape(ATTENTION_PLANES, DH)
    inputs = (query_rows.reshape(blocks, TOK_DEV, ATTENTION_PLANES, DH), key_rows.reshape(blocks, TOK_DEV, ATTENTION_PLANES, DH), value_rows.reshape(blocks, TOK_DEV, ATTENTION_PLANES, DH), log_decay.reshape(blocks, TOK_DEV, ATTENTION_PLANES), doc_ids.reshape(blocks, TOK_DEV), prev_docs)

    def block_step(carry_state, items):
        queries, key_block, value_block, decay_block, block_docs, prev_doc = items
        within, decayed_queries, carried, end_log, opened, block_state = block_terms(queries, key_block, value_block, decay_block, block_docs, prev_doc)
        normed = finish(within, decayed_queries, carried, carry_state, gain_heads)
        new_state = block_state + ((1.0 - opened) * jnp.exp(end_log))[:, None, None] * carry_state
        return (new_state, normed)
    start_state = jnp.zeros((ATTENTION_PLANES, DH, DH), jnp.float32)
    last_state, outputs = lax.scan(block_step, start_state, inputs)
    return outputs.reshape(SEQUENCE_SYMBOLS, ATTENTION_PLANES * DH)
```

```python
import functools
import math

import jax
import jax.numpy as jnp
from jax import lax
from jax.experimental import pallas as pl
from jax.experimental.pallas import tpu as pltpu
from jax.sharding import PartitionSpec as P

MESH = pl.DeviceIdType.MESH
LOG2E = math.log2(math.e)
OFF = -1e30
TILE = 128
EXTRA = 16


def kernel(
    n_seq, n_sec, levels,
    q_ref, k_ref, v_ref, decay_ref, len_ref, gain_ref,
    out_ref,
    cum, kept, in_last, bias, carry_bias, entry, factor, within, state,
    msg, inbox, rows_out,
    msg_send, msg_recv, out_send, out_recv, own_sem,
):
    tok = q_ref.shape[0]
    heads, _ = decay_ref.shape
    size = TILE
    tiles = tok // TILE
    me, sec = lax.axis_index("seq"), lax.axis_index("section")
    out_rows = tok // n_sec

    quarter = n_seq // 4
    first = jnp.where(me < quarter, 0, jnp.where(me < n_seq - quarter, quarter, n_seq - quarter))
    span = jnp.where((me >= quarter) & (me < n_seq - quarter), n_seq - 2 * quarter, quarter)
    place = me - first
    has_next = place + 1 < span

    def sends(level):
        return has_next & (lax.rem(place, 2 ** (level + 1)) == 2**level - 1)

    def before(level):
        return has_next & (lax.rem(place, 2 ** (level + 1)) == 2 ** (level + 1) - 1)

    def receives(level):
        return lax.rem(lax.div(place, 2**level), 2) == 1

    def source(level):
        return first + lax.div(place, 2**level) * 2**level - 1

    def targets(level):
        return range(1, 2**level + 1)

    barrier = pltpu.get_barrier_semaphore()
    partners = jnp.int32(n_sec - 1)
    for level in range(levels):
        @pl.when(receives(level))
        def _():
            pl.semaphore_signal(
                barrier, inc=1, device_id=(source(level), sec), device_id_type=MESH
            )
        partners = partners + jnp.where(receives(level), 1, 0)
        for step in targets(level):
            reach = sends(level) & (place + step < span)

            @pl.when(reach)
            def _():
                pl.semaphore_signal(
                    barrier, inc=1, device_id=(me + step, sec), device_id_type=MESH
                )
            partners = partners + jnp.where(reach, 1, 0)
    for step in range(1, n_sec):
        pl.semaphore_signal(
            barrier, inc=1, device_id=(me, lax.rem(sec + step, n_sec)), device_id_type=MESH
        )

    row0 = me * tok
    pos = row0 + lax.broadcasted_iota(jnp.int32, (1, tok), 1)
    ids = jnp.zeros((1, tok), jnp.int32)
    end = jnp.int32(0)
    prev_doc = jnp.int32(0)
    last_doc = jnp.int32(0)
    for doc in range(len_ref.shape[0]):
        end = end + len_ref[doc]
        ids = ids + jnp.where(pos >= end, 1, 0)
        prev_doc = prev_doc + jnp.where(end <= row0 - 1, 1, 0)
        last_doc = last_doc + jnp.where(end <= row0 + tok - 1, 1, 0)
    stays = jnp.where(last_doc == prev_doc, 1.0, 0.0).astype(jnp.float32)
    in_last[...] = jnp.where(ids == last_doc, 1.0, 0.0)
    ids_f = ids.astype(jnp.float32)
    log_scale = -0.5 * math.log2(size)
    low = lax.broadcasted_iota(jnp.int32, (TILE, TILE), 0)
    col = lax.broadcasted_iota(jnp.int32, (TILE, TILE), 1)
    prev_f = prev_doc.astype(jnp.float32)
    for i in range(tiles):
        mine = slice(i * TILE, (i + 1) * TILE)
        ids_col = jnp.broadcast_to(ids_f[:, mine], (TILE, TILE)).T
        carry_bias[mine, :] = jnp.where(ids_col == prev_f, log_scale, OFF)
        for j in range(i + 1):
            theirs = slice(j * TILE, (j + 1) * TILE)
            ok = ids_col == ids_f[:, theirs]
            if i == j:
                ok = ok & (low >= col)
            bias[mine, theirs] = jnp.where(ok, log_scale, OFF)

    upto = (
        lax.broadcasted_iota(jnp.int32, (tok, tok), 0)
        <= lax.broadcasted_iota(jnp.int32, (tok, tok), 1)
    )
    upto = jnp.where(upto, 1.0, 0.0).astype(jnp.bfloat16)
    rest = decay_ref[...]
    total = jnp.zeros((heads, tok), jnp.float32)
    for _ in range(3):
        part = rest.astype(jnp.bfloat16)
        total = total + jnp.dot(part, upto, preferred_element_type=jnp.float32)
        rest = rest - part.astype(jnp.float32)
    total = total * LOG2E
    cum[...] = total
    kept[...] = jnp.broadcast_to(jnp.exp2(total[:, tok - 1 :]) * stays, (heads, TILE))

    pl.semaphore_wait(barrier, partners)

    def message(head, level, step):
        return pltpu.make_async_remote_copy(
            src_ref=msg.at[head],
            dst_ref=inbox.at[level, head],
            send_sem=msg_send.at[step - 1, head],
            recv_sem=msg_recv.at[level, head],
            device_id=(me + step, sec),
            device_id_type=MESH,
        )

    def arrive(head, level):
        pltpu.make_async_remote_copy(
            src_ref=msg.at[head],
            dst_ref=inbox.at[level, head],
            send_sem=msg_send.at[0, head],
            recv_sem=msg_recv.at[level, head],
            device_id=(source(level), sec),
            device_id_type=MESH,
        ).wait_recv()
        block = inbox[level, head]
        entry[...] = entry[...] + factor[...] * block[:size].astype(jnp.float32)
        high = block[size : size + 1].astype(jnp.float32)
        factor[...] = factor[...] * (high + block[size + 8 : size + 9].astype(jnp.float32))

    def outgoing(head, step):
        to = lax.rem(sec + step, n_sec)
        return pltpu.make_async_remote_copy(
            src_ref=rows_out.at[head, pl.ds(to * out_rows, out_rows), :],
            dst_ref=out_ref.at[:, pl.ds(pl.multiple_of((sec * heads + head) * size, size), size)],
            send_sem=out_send.at[step - 1, head],
            recv_sem=out_recv.at[step - 1, head],
            device_id=(me, to),
            device_id_type=MESH,
        )

    def incoming(head, step):
        by = lax.rem(sec + n_sec - step, n_sec)
        return pltpu.make_async_remote_copy(
            src_ref=rows_out.at[head, pl.ds(by * out_rows, out_rows), :],
            dst_ref=out_ref.at[:, pl.ds(pl.multiple_of((by * heads + head) * size, size), size)],
            send_sem=out_send.at[step - 1, head],
            recv_sem=out_recv.at[step - 1, head],
            device_id=(me, by),
            device_id_type=MESH,
        )

    def own(head):
        return pltpu.make_async_copy(
            rows_out.at[head, pl.ds(sec * out_rows, out_rows), :],
            out_ref.at[:, pl.ds(pl.multiple_of((sec * heads + head) * size, size), size)],
            own_sem.at[head],
        )

    def one_head(head, carry):
        at = pl.ds(pl.multiple_of(head * size, size), size)
        row = cum[pl.ds(head, 1), :]
        k_turned = k_ref[:, at].T
        v_head = v_ref[:, at]
        to_end = jnp.exp2(row[:, tok - 1 :] - row) * in_last[...]
        decayed = (k_turned.astype(jnp.float32) * to_end).astype(jnp.bfloat16)
        state[...] = jnp.dot(decayed, v_head, preferred_element_type=jnp.float32)
        entry[...] = jnp.zeros_like(entry)
        factor[...] = jnp.ones_like(factor)
        for level in range(levels):
            @pl.when(sends(level))
            def _():
                keep = kept[pl.ds(head, 1), :]
                msg[head, :size, :] = (state[...] + keep * entry[...]).astype(jnp.bfloat16)
                through = keep * factor[...]
                high = through.astype(jnp.bfloat16)
                low_part = (through - high.astype(jnp.float32)).astype(jnp.bfloat16)
                msg[head, size:, :] = jnp.concatenate(
                    [
                        jnp.broadcast_to(high.astype(jnp.float32), (8, TILE)),
                        jnp.broadcast_to(low_part.astype(jnp.float32), (8, TILE)),
                    ]
                ).astype(jnp.bfloat16)
                for step in targets(level):
                    @pl.when(place + step < span)
                    def _():
                        message(head, level, step).start()

            @pl.when(before(level))
            def _():
                arrive(head, level)

        cols = []
        for i in range(tiles):
            mine = slice(i * TILE, (i + 1) * TILE)
            cum_col = jnp.broadcast_to(row[:, mine], (TILE, TILE)).T
            cols.append(cum_col)
            width = (i + 1) * TILE
            scores = jnp.dot(
                q_ref[mine, at], k_turned[:, :width], preferred_element_type=jnp.float32
            )
            weights = []
            for j in range(i + 1):
                theirs = slice(j * TILE, (j + 1) * TILE)
                gap = (cum_col - row[:, theirs]) + bias[mine, theirs]
                weights.append((scores[:, theirs] * jnp.exp2(gap)).astype(jnp.bfloat16))
            weights = jnp.concatenate(weights, axis=1) if i else weights[0]
            within[mine, :] = jnp.dot(
                weights, v_head[:width], preferred_element_type=jnp.float32
            )

        for level in range(levels):
            @pl.when(receives(level) & jnp.logical_not(before(level)))
            def _():
                arrive(head, level)

        before_block = entry[...].astype(jnp.bfloat16)
        gain = gain_ref[pl.ds(head, 1), :]
        for i in range(tiles):
            mine = slice(i * TILE, (i + 1) * TILE)
            carried = jnp.dot(q_ref[mine, at], before_block, preferred_element_type=jnp.float32)
            attention = within[mine, :] + carried * jnp.exp2(cols[i] + carry_bias[mine, :])
            mean_square = jnp.mean(attention * attention, axis=-1, keepdims=True)
            normed = attention * lax.rsqrt(mean_square + 1e-05) * gain
            rows_out[head, mine, :] = normed.astype(jnp.bfloat16)
        for step in range(1, n_sec):
            outgoing(head, step).start()
        own(head).start()
        return carry

    lax.fori_loop(0, heads, one_head, 0)

    def drain(head, carry):
        for level in range(levels):
            for step in targets(level):
                @pl.when(sends(level) & (place + step < span))
                def _():
                    message(head, level, step).wait_send()
        own(head).wait()
        for step in range(1, n_sec):
            outgoing(head, step).wait_send()
            incoming(head, step).wait_recv()
        return carry

    lax.fori_loop(0, heads, drain, 0)


def shards(n_seq, n_sec, query_rows, key_rows, value_rows, log_decay, lengths, norm_gain):
    tok, width = query_rows.shape
    heads = log_decay.shape[1]
    size = width // heads
    longest = max(n_seq - 2 * (n_seq // 4), 1)
    levels = max((longest - 1).bit_length(), 1)
    fan = 2 ** (levels - 1)
    vmem = pl.BlockSpec(memory_space=pltpu.VMEM)
    return pl.pallas_call(
        functools.partial(kernel, n_seq, n_sec, levels),
        out_shape=jax.ShapeDtypeStruct((tok // n_sec, width * n_sec), jnp.bfloat16),
        in_specs=[vmem] * 4 + [pl.BlockSpec(memory_space=pltpu.SMEM), vmem],
        out_specs=pl.BlockSpec(memory_space=pl.ANY),
        scratch_shapes=[
            pltpu.VMEM((heads, tok), jnp.float32),
            pltpu.VMEM((heads, TILE), jnp.float32),
            pltpu.VMEM((1, tok), jnp.float32),
            pltpu.VMEM((tok, tok), jnp.float32),
            pltpu.VMEM((tok, TILE), jnp.float32),
            pltpu.VMEM((size, size), jnp.float32),
            pltpu.VMEM((1, size), jnp.float32),
            pltpu.VMEM((tok, size), jnp.float32),
            pltpu.VMEM((size, size), jnp.float32),
            pltpu.VMEM((heads, size + EXTRA, size), jnp.bfloat16),
            pltpu.VMEM((levels, heads, size + EXTRA, size), jnp.bfloat16),
            pltpu.VMEM((heads, tok, size), jnp.bfloat16),
            pltpu.SemaphoreType.DMA((fan, heads)),
            pltpu.SemaphoreType.DMA((levels, heads)),
            pltpu.SemaphoreType.DMA((max(n_sec - 1, 1), heads)),
            pltpu.SemaphoreType.DMA((max(n_sec - 1, 1), heads)),
            pltpu.SemaphoreType.DMA((heads,)),
        ],
        compiler_params=pltpu.CompilerParams(
            collective_id=0, has_side_effects=True, vmem_limit_bytes=40 * 1024 * 1024
        ),
        cost_estimate=pl.CostEstimate(
            flops=2 * heads * tok * size * (tok + 2 * size),
            bytes_accessed=8 * tok * width,
            transcendentals=heads * tok * tok,
        ),
    )(query_rows, key_rows, value_rows, log_decay.T, lengths, norm_gain.reshape(heads, size))


def solution(mesh):
    rows = P("seq", "section")
    return jax.shard_map(
        functools.partial(shards, mesh.shape["seq"], mesh.shape["section"]),
        mesh=mesh,
        in_specs=(rows, rows, rows, rows, P(), P("section")),
        out_specs=P(("seq", "section"), None),
        check_vma=False,
    )
```

```python
import functools
import math

import jax
import jax.numpy as jnp
from jax import lax
from jax.experimental import pallas as pl
from jax.experimental.pallas import tpu as pltpu
from jax.sharding import PartitionSpec as P

MESH = pl.DeviceIdType.MESH
LOG2E = math.log2(math.e)
OFF = -1e30
TILE = 128
EXTRA = 16
AHEAD = 3


def kernel(
    n_seq, n_sec, levels,
    q_hbm, k_hbm, v_hbm, decay_hbm, len_hbm, gain_hbm,
    out_ref,
    q_buf, k_buf, v_buf, decay_ref, len_ref, gain_ref,
    cum, kept, in_last, bias, carry_bias, entry, factor, within, state,
    msg, inbox, rows_out,
    msg_send, msg_recv, relay_send, out_send, out_recv, own_sem, in_sem, small_sem,
):
    tok = q_hbm.shape[0]
    heads, _ = decay_ref.shape
    size = TILE
    tiles = tok // TILE
    relayed = 2 if n_seq % 8 == 0 else levels

    small = [
        pltpu.make_async_copy(decay_hbm, decay_ref, small_sem.at[0]),
        pltpu.make_async_copy(len_hbm, len_ref, small_sem.at[1]),
        pltpu.make_async_copy(gain_hbm, gain_ref, small_sem.at[2]),
    ]
    for copy in small:
        copy.start()

    def load(head):
        at = pl.ds(pl.multiple_of(head * size, size), size)
        return [
            pltpu.make_async_copy(whole.at[:, at], part.at[head], in_sem.at[which, head])
            for which, (whole, part) in enumerate(((k_hbm, k_buf), (v_hbm, v_buf), (q_hbm, q_buf)))
        ]

    ahead = min(AHEAD, heads)
    for head in range(ahead):
        for copy in load(head):
            copy.start()

    me, sec = lax.axis_index("seq"), lax.axis_index("section")
    out_rows = tok // n_sec

    quarter = n_seq // 4
    first = jnp.where(me < quarter, 0, jnp.where(me < n_seq - quarter, quarter, n_seq - quarter))
    span = jnp.where((me >= quarter) & (me < n_seq - quarter), n_seq - 2 * quarter, quarter)
    place = me - first
    has_next = place + 1 < span

    def sends(level):
        return has_next & (lax.rem(place, 2 ** (level + 1)) == 2**level - 1)

    def before(level):
        return has_next & (lax.rem(place, 2 ** (level + 1)) == 2 ** (level + 1) - 1)

    def receives(level):
        return lax.rem(lax.div(place, 2**level), 2) == 1

    odd = lax.rem(place, 2) == 1

    def source(level):
        block = first + lax.div(place, 2**level) * 2**level - 1
        return jnp.where(odd, block, me + 1) if level >= relayed else block

    def targets(level):
        return range(2**level, 0, -2 if level >= relayed else -1)

    barrier = pltpu.get_barrier_semaphore()
    partners = jnp.int32(n_sec - 1)
    for level in range(levels):
        @pl.when(receives(level))
        def _():
            pl.semaphore_signal(
                barrier, inc=1, device_id=(source(level), sec), device_id_type=MESH
            )
        partners = partners + jnp.where(receives(level), 1, 0)
        if level >= relayed:
            @pl.when(receives(level) & odd)
            def _():
                pl.semaphore_signal(barrier, inc=1, device_id=(me - 1, sec), device_id_type=MESH)
            partners = partners + jnp.where(receives(level) & odd, 1, 0)
        for step in targets(level):
            reach = sends(level) & (place + step < span)

            @pl.when(reach)
            def _():
                pl.semaphore_signal(
                    barrier, inc=1, device_id=(me + step, sec), device_id_type=MESH
                )
            partners = partners + jnp.where(reach, 1, 0)
    for step in range(1, n_sec):
        pl.semaphore_signal(
            barrier, inc=1, device_id=(me, lax.rem(sec + step, n_sec)), device_id_type=MESH
        )

    for copy in small:
        copy.wait()

    row0 = me * tok
    pos = row0 + lax.broadcasted_iota(jnp.int32, (1, tok), 1)
    ids = jnp.zeros((1, tok), jnp.int32)
    end = jnp.int32(0)
    prev_doc = jnp.int32(0)
    last_doc = jnp.int32(0)
    for doc in range(len_ref.shape[0]):
        end = end + len_ref[doc]
        ids = ids + jnp.where(pos >= end, 1, 0)
        prev_doc = prev_doc + jnp.where(end <= row0 - 1, 1, 0)
        last_doc = last_doc + jnp.where(end <= row0 + tok - 1, 1, 0)
    stays = jnp.where(last_doc == prev_doc, 1.0, 0.0).astype(jnp.float32)
    in_last[...] = jnp.where(ids == last_doc, 1.0, 0.0)
    ids_f = ids.astype(jnp.float32)
    log_scale = -0.5 * math.log2(size)
    low = lax.broadcasted_iota(jnp.int32, (TILE, TILE), 0)
    col = lax.broadcasted_iota(jnp.int32, (TILE, TILE), 1)
    prev_f = prev_doc.astype(jnp.float32)
    for i in range(tiles):
        mine = slice(i * TILE, (i + 1) * TILE)
        ids_col = jnp.broadcast_to(ids_f[:, mine], (TILE, TILE)).T
        carry_bias[mine, :] = jnp.where(ids_col == prev_f, log_scale, OFF)
        for j in range(i + 1):
            theirs = slice(j * TILE, (j + 1) * TILE)
            ok = ids_col == ids_f[:, theirs]
            if i == j:
                ok = ok & (low >= col)
            bias[mine, theirs] = jnp.where(ok, log_scale, OFF)

    upto = (
        lax.broadcasted_iota(jnp.int32, (tok, tok), 0)
        <= lax.broadcasted_iota(jnp.int32, (tok, tok), 1)
    )
    upto = jnp.where(upto, 1.0, 0.0).astype(jnp.bfloat16)
    rest = decay_ref[...]
    total = jnp.zeros((heads, tok), jnp.float32)
    for _ in range(3):
        part = rest.astype(jnp.bfloat16)
        total = total + jnp.dot(part, upto, preferred_element_type=jnp.float32)
        rest = rest - part.astype(jnp.float32)
    total = total * LOG2E
    cum[...] = total
    kept[...] = jnp.broadcast_to(jnp.exp2(total[:, tok - 1 :]) * stays, (heads, TILE))

    pl.semaphore_wait(barrier, partners)

    def message(head, level, step):
        return pltpu.make_async_remote_copy(
            src_ref=msg.at[head],
            dst_ref=inbox.at[level, head],
            send_sem=msg_send.at[step - 1, head],
            recv_sem=msg_recv.at[level, head],
            device_id=(me + step, sec),
            device_id_type=MESH,
        )

    def relay(head, level):
        return pltpu.make_async_remote_copy(
            src_ref=inbox.at[level, head],
            dst_ref=inbox.at[level, head],
            send_sem=relay_send.at[level, head],
            recv_sem=msg_recv.at[level, head],
            device_id=(me - 1, sec),
            device_id_type=MESH,
        )

    def arrive(head, level):
        pltpu.make_async_remote_copy(
            src_ref=msg.at[head],
            dst_ref=inbox.at[level, head],
            send_sem=msg_send.at[0, head],
            recv_sem=msg_recv.at[level, head],
            device_id=(source(level), sec),
            device_id_type=MESH,
        ).wait_recv()
        if level >= relayed:
            @pl.when(odd)
            def _():
                relay(head, level).start()
        block = inbox[level, head]
        entry[...] = entry[...] + factor[...] * block[:size].astype(jnp.float32)
        high = block[size : size + 1].astype(jnp.float32)
        factor[...] = factor[...] * (high + block[size + 8 : size + 9].astype(jnp.float32))

    def outgoing(head, step):
        to = lax.rem(sec + step, n_sec)
        return pltpu.make_async_remote_copy(
            src_ref=rows_out.at[head, pl.ds(to * out_rows, out_rows), :],
            dst_ref=out_ref.at[:, pl.ds(pl.multiple_of((sec * heads + head) * size, size), size)],
            send_sem=out_send.at[step - 1, head],
            recv_sem=out_recv.at[step - 1, head],
            device_id=(me, to),
            device_id_type=MESH,
        )

    def incoming(head, step):
        by = lax.rem(sec + n_sec - step, n_sec)
        return pltpu.make_async_remote_copy(
            src_ref=rows_out.at[head, pl.ds(by * out_rows, out_rows), :],
            dst_ref=out_ref.at[:, pl.ds(pl.multiple_of((by * heads + head) * size, size), size)],
            send_sem=out_send.at[step - 1, head],
            recv_sem=out_recv.at[step - 1, head],
            device_id=(me, by),
            device_id_type=MESH,
        )

    def own(head):
        return pltpu.make_async_copy(
            rows_out.at[head, pl.ds(sec * out_rows, out_rows), :],
            out_ref.at[:, pl.ds(pl.multiple_of((sec * heads + head) * size, size), size)],
            own_sem.at[head],
        )

    def one_head(head, carry):
        @pl.when(head + ahead < heads)
        def _():
            for copy in load(head + ahead):
                copy.start()

        row = cum[pl.ds(head, 1), :]
        k_load, v_load, q_load = load(head)
        k_load.wait()
        v_load.wait()
        k_turned = k_buf[head].T
        v_head = v_buf[head]
        to_end = jnp.exp2(row[:, tok - 1 :] - row) * in_last[...]
        decayed = (k_turned.astype(jnp.float32) * to_end).astype(jnp.bfloat16)
        state[...] = jnp.dot(decayed, v_head, preferred_element_type=jnp.float32)
        entry[...] = jnp.zeros_like(entry)
        factor[...] = jnp.ones_like(factor)
        for level in range(levels):
            @pl.when(sends(level))
            def _():
                keep = kept[pl.ds(head, 1), :]
                msg[head, :size, :] = (state[...] + keep * entry[...]).astype(jnp.bfloat16)
                through = keep * factor[...]
                high = through.astype(jnp.bfloat16)
                low_part = (through - high.astype(jnp.float32)).astype(jnp.bfloat16)
                msg[head, size:, :] = jnp.concatenate(
                    [
                        jnp.broadcast_to(high.astype(jnp.float32), (8, TILE)),
                        jnp.broadcast_to(low_part.astype(jnp.float32), (8, TILE)),
                    ]
                ).astype(jnp.bfloat16)
                for step in targets(level):
                    @pl.when(place + step < span)
                    def _():
                        message(head, level, step).start()

            @pl.when(before(level))
            def _():
                arrive(head, level)

        q_load.wait()
        cols = []
        for i in range(tiles):
            mine = slice(i * TILE, (i + 1) * TILE)
            cum_col = jnp.broadcast_to(row[:, mine], (TILE, TILE)).T
            cols.append(cum_col)
            width = (i + 1) * TILE
            scores = jnp.dot(
                q_buf[head, mine, :], k_turned[:, :width], preferred_element_type=jnp.float32
            )
            weights = []
            for j in range(i + 1):
                theirs = slice(j * TILE, (j + 1) * TILE)
                gap = (cum_col - row[:, theirs]) + bias[mine, theirs]
                weights.append((scores[:, theirs] * jnp.exp2(gap)).astype(jnp.bfloat16))
            weights = jnp.concatenate(weights, axis=1) if i else weights[0]
            within[mine, :] = jnp.dot(
                weights, v_head[:width], preferred_element_type=jnp.float32
            )

        for level in range(levels):
            @pl.when(receives(level) & jnp.logical_not(before(level)))
            def _():
                arrive(head, level)

        before_block = entry[...].astype(jnp.bfloat16)
        gain = gain_ref[pl.ds(head, 1), :]
        for i in range(tiles):
            mine = slice(i * TILE, (i + 1) * TILE)
            carried = jnp.dot(
                q_buf[head, mine, :], before_block, preferred_element_type=jnp.float32
            )
            attention = within[mine, :] + carried * jnp.exp2(cols[i] + carry_bias[mine, :])
            mean_square = jnp.mean(attention * attention, axis=-1, keepdims=True)
            normed = attention * lax.rsqrt(mean_square + 1e-05) * gain
            rows_out[head, mine, :] = normed.astype(jnp.bfloat16)
        for step in range(1, n_sec):
            outgoing(head, step).start()
        own(head).start()
        return carry

    lax.fori_loop(0, heads, one_head, 0)

    def drain(head, carry):
        for level in range(levels):
            for step in targets(level):
                @pl.when(sends(level) & (place + step < span))
                def _():
                    message(head, level, step).wait_send()
            if level >= relayed:
                @pl.when(receives(level) & odd)
                def _():
                    relay(head, level).wait_send()
        own(head).wait()
        for step in range(1, n_sec):
            outgoing(head, step).wait_send()
            incoming(head, step).wait_recv()
        return carry

    lax.fori_loop(0, heads, drain, 0)


def shards(n_seq, n_sec, query_rows, key_rows, value_rows, log_decay, lengths, norm_gain):
    tok, width = query_rows.shape
    heads = log_decay.shape[1]
    size = width // heads
    longest = max(n_seq - 2 * (n_seq // 4), 1)
    levels = max((longest - 1).bit_length(), 1)
    fan = 2 ** (levels - 1)
    hbm = pl.BlockSpec(memory_space=pltpu.HBM)
    return pl.pallas_call(
        functools.partial(kernel, n_seq, n_sec, levels),
        out_shape=jax.ShapeDtypeStruct((tok // n_sec, width * n_sec), jnp.bfloat16),
        in_specs=[hbm] * 6,
        out_specs=pl.BlockSpec(memory_space=pl.ANY),
        scratch_shapes=[
            pltpu.VMEM((heads, tok, size), jnp.bfloat16),
            pltpu.VMEM((heads, tok, size), jnp.bfloat16),
            pltpu.VMEM((heads, tok, size), jnp.bfloat16),
            pltpu.VMEM((heads, tok), jnp.float32),
            pltpu.SMEM(lengths.shape, jnp.int32),
            pltpu.VMEM((heads, size), jnp.float32),
            pltpu.VMEM((heads, tok), jnp.float32),
            pltpu.VMEM((heads, TILE), jnp.float32),
            pltpu.VMEM((1, tok), jnp.float32),
            pltpu.VMEM((tok, tok), jnp.float32),
            pltpu.VMEM((tok, TILE), jnp.float32),
            pltpu.VMEM((size, size), jnp.float32),
            pltpu.VMEM((1, size), jnp.float32),
            pltpu.VMEM((tok, size), jnp.float32),
            pltpu.VMEM((size, size), jnp.float32),
            pltpu.VMEM((heads, size + EXTRA, size), jnp.bfloat16),
            pltpu.VMEM((levels, heads, size + EXTRA, size), jnp.bfloat16),
            pltpu.VMEM((heads, tok, size), jnp.bfloat16),
            pltpu.SemaphoreType.DMA((fan, heads)),
            pltpu.SemaphoreType.DMA((levels, heads)),
            pltpu.SemaphoreType.DMA((levels, heads)),
            pltpu.SemaphoreType.DMA((max(n_sec - 1, 1), heads)),
            pltpu.SemaphoreType.DMA((max(n_sec - 1, 1), heads)),
            pltpu.SemaphoreType.DMA((heads,)),
            pltpu.SemaphoreType.DMA((3, heads)),
            pltpu.SemaphoreType.DMA((3,)),
        ],
        compiler_params=pltpu.CompilerParams(
            collective_id=0, has_side_effects=True, vmem_limit_bytes=59 * 1024 * 1024
        ),
        cost_estimate=pl.CostEstimate(
            flops=2 * heads * tok * size * (tok + 2 * size),
            bytes_accessed=8 * tok * width,
            transcendentals=heads * tok * tok,
        ),
    )(query_rows, key_rows, value_rows, log_decay.T, lengths, norm_gain.reshape(heads, size))


def solution(mesh):
    rows = P("seq", "section")
    return jax.shard_map(
        functools.partial(shards, mesh.shape["seq"], mesh.shape["section"]),
        mesh=mesh,
        in_specs=(rows, rows, rows, rows, P(), P("section")),
        out_specs=P(("seq", "section"), None),
        check_vma=False,
    )
```
